512 devices in a mesh: section: 4 (over x), seq: 16 (over z), tp: 8 (over y, core).
Axes of the slice: x: 4, y: 4, z: 16, core: 2. Of those that a mesh axis runs over, the one named last changes fastest.
Arguments:
- merged_hidden: bfloat16 [3072, 5120], P('section', 'seq'), may hold values from -6 to 6
- merger_weight: bfloat16 [5120, 8192], P('seq', 'tp'), may hold values from -0.078125 to 0.078125
- merger_bias: float32 [8192], P('tp'), may hold values from -3 to 3
- text_embed: bfloat16 [16384, 8192], P(('section', 'seq'), 'tp'), may hold values from -108 to 108
- image_tokens: int32 [64, 4], P(('section', 'seq')), may hold values from 1 to 45, as said below
- image_offsets: int32 [64, 4], P(('section', 'seq')), may hold values from 1 to 191, as said below
- prefill_gain: bfloat16 [8192], P('tp'), may hold values from 0.099609375 to 1.8984375
- kv_weight: bfloat16 [8192, 2048], P('seq', 'tp'), may hold values from -0.0625 to 0.0625
- kv_bias: float32 [2048], P('tp'), may hold values from -4 to 4
- prompt_lengths: int32 [64], replicated, may hold values from 193 to 256, as said below
- queries: bfloat16 [1024, 8192], P(('section', 'seq'), 'tp'), may hold values from -5 to 5
- cache_pages: bfloat16 [15360, 16, 2048], P(('section', 'seq'), None, 'tp'), may hold values from -5 to 5
- page_tables: int32 [960, 16], P(('section', 'seq')), may hold values from 0 to 239, as said below
- context_lengths: int32 [960], P(('section', 'seq')), may hold values from 2 to 256, as said below
Outputs:
- prompt_cache: bfloat16 [16384, 2048], P(('section', 'seq'), 'tp')
- decode_out: bfloat16 [1024, 8192], P(('section', 'seq'), 'tp')
The draws below stay inside these ranges and needn't reach their ends.
Inputs may be any that keep to these rules, and one draw needn't show every extreme that they name: `image_tokens`: each prompt's image token counts sum to 48. `image_offsets`: images of a prompt lie in order and apart, within its first 192 positions. `prompt_lengths`: some prompt has 256 tokens; every image of a prompt ends before its length. `context_lengths`: some request has 256 cached positions. `page_tables`: the pages of one owner's resident requests are distinct pages of that owner's block.
All inputs are finite; a program needn't handle non-finite values.
Results may differ from the reference program's by a relative error of at most 0.0047.
Values may be sent and summed in bfloat16 or wider, within the bound.
No kernel may reach another device: no remote copies, remote signals or barrier semaphores. Data moves between devices by JAX's collectives and lax.ppermute only.
A program may use at most 64 MiB of HBM per device.

```python
import math
import jax
import jax.numpy as jnp
from jax import lax

D = 8192
QH = 64
KVH = 8
HD = 128
PAGE = 16
IMG = 4
MD = 48
PL = 256
RQ = 15
QPK = 8
MW = 5120
PROMPTS = 64
MAXP = 16
POOL = 240
N_SEQ = 16


def image_layout(key):
    key = jax.random.fold_in(key, 101)
    cut_key, gap_key, pick_key = jax.random.split(key, 3)

    def cut_points(sub_key):
        chosen = jax.random.permutation(sub_key, MD - 1)[:IMG - 1] + 1
        return jnp.sort(chosen).astype(jnp.int32)
    cut_marks = jax.vmap(cut_points)(jax.random.split(cut_key, PROMPTS))
    selected = jax.random.randint(pick_key, (), 0, PROMPTS)
    second = (selected + 1) % PROMPTS
    row_ids = jnp.arange(PROMPTS)[:, None]
    column_ids = jnp.arange(IMG)[None, :]
    forced_cuts = (MD - IMG + 1 + jnp.arange(IMG - 1)).astype(jnp.int32)[None, :]
    cut_marks = jnp.where(row_ids == selected, forced_cuts, cut_marks).astype(jnp.int32)
    boundary = jnp.concatenate([jnp.zeros((PROMPTS, 1), jnp.int32), cut_marks, jnp.full((PROMPTS, 1), MD, jnp.int32)], axis=1)
    token_counts = boundary[:, 1:] - boundary[:, :-1]
    widest = (3 * PL // 4 - MD) // IMG + 1
    gap_sizes = jax.random.randint(gap_key, (PROMPTS, IMG), 1, widest)
    gap_sizes = jnp.where(row_ids == selected, widest - 1, gap_sizes)
    gap_sizes = jnp.where((row_ids == second) & (column_ids == 0), 1, gap_sizes)
    start_rows = jnp.cumsum(gap_sizes, axis=1) + jnp.cumsum(token_counts, axis=1) - token_counts
    return (token_counts.astype(jnp.int32), start_rows.astype(jnp.int32))


def page_order(key):
    key = jax.random.fold_in(key, 23)

    def one_block(sub_key):
        return jax.random.permutation(sub_key, POOL).astype(jnp.int32)
    return jax.vmap(one_block)(jax.random.split(key, PROMPTS))


def draw_image_tokens(key, part):
    token_counts, start_rows = image_layout(key)
    return token_counts


def draw_image_offsets(key, part):
    token_counts, start_rows = image_layout(key)
    return start_rows


def draw_prompt_lengths(key, part):
    key = jax.random.fold_in(key, 7)
    short_key, pick_key = jax.random.split(key)
    lengths_drawn = PL - jax.random.randint(short_key, (PROMPTS,), 0, PL // 4)
    longest = jax.random.randint(pick_key, (), 0, PROMPTS)
    return jnp.where(jnp.arange(PROMPTS) == longest, PL, lengths_drawn).astype(jnp.int32)


def draw_context_lengths(key, part):
    key = jax.random.fold_in(key, 13)
    span_key, pick_key = jax.random.split(key)
    lengths_drawn = jax.random.randint(span_key, (PROMPTS * RQ,), 2, PL + 1)
    longest = jax.random.randint(pick_key, (), 0, PROMPTS * RQ)
    return jnp.where(jnp.arange(PROMPTS * RQ) == longest, PL, lengths_drawn).astype(jnp.int32)


def draw_page_tables(key, part):
    return page_order(key).reshape(PROMPTS * RQ, MAXP)


def draw_text_embed(key, part):
    key = jax.random.fold_in(key, 41)
    value_key, row_key = jax.random.split(key)
    column_pos = jnp.arange(D, dtype=jnp.float32)[None, :] / D
    row_pos = jax.random.uniform(row_key, (PROMPTS * PL, 1), jnp.float32, 0.0, 1.0)
    row_scale = 10.0 ** (row_pos - 0.5)
    base = jnp.clip(jax.random.normal(value_key, (PROMPTS * PL, D), jnp.float32), -3.0, 3.0) * 10.0 ** column_pos
    return (base * row_scale).astype(jnp.bfloat16)


def draw_queries(key, part):
    key = jax.random.fold_in(key, 59)
    value_key = jax.random.fold_in(key, 0)
    shape = (PROMPTS, RQ + 1, KVH, QPK, HD)
    base = jnp.clip(jax.random.normal(value_key, shape, jnp.float32), -5.0, 5.0)
    return base.reshape(PROMPTS * (RQ + 1), QH * HD).astype(jnp.bfloat16)


def draw_cache_pages(key, part):
    key = jax.random.fold_in(key, 53)
    value_key = jax.random.fold_in(key, 0)
    shape = (PROMPTS, POOL, PAGE, KVH, 2, HD)
    base = jnp.clip(jax.random.normal(value_key, shape, jnp.float32), -5.0, 5.0)
    return base.reshape(PROMPTS * POOL, PAGE, 2 * HD * KVH).astype(jnp.bfloat16)


def shard_levels(key, dims, cuts, least, top_value):
    factor_of, own = 1.0, jax.random.fold_in(key, 6)
    for dim, blocks in cuts:
        heights = jnp.exp(jax.random.uniform(jax.random.fold_in(own, dim), (blocks,), jnp.float32, least / len(cuts), top_value / len(cuts)))
        factor_of = factor_of * jnp.repeat(heights, dims[dim] // blocks).reshape([-1 if axis == dim else 1 for axis in range(len(dims))])
    return factor_of


def centred(key, dims, spread, bound, shards=(), kind=jnp.bfloat16):
    drawn = spread * jax.random.normal(key, dims, jnp.float32)
    if shards:
        drawn = drawn * shard_levels(key, dims, shards, -0.22, 0.18)
    return jnp.clip(drawn, -bound, bound).astype(kind)


def setup_inputs(seed: int = 0) -> dict:
    streams_of = jax.random.split(jax.random.key(seed), 15)
    merged_hidden = centred(streams_of[0], (PROMPTS * MD, MW), 1.0, 6.0, ((0, 4), (1, 16)))
    merger_weight = centred(streams_of[1], (MW, D), MW ** -0.5, 0.078125, ((0, 16), (1, 8)))
    merger_bias = centred(streams_of[2], (D,), 0.5, 3.0, ((0, 8),), jnp.float32)
    text_embed = draw_text_embed(jax.random.fold_in(streams_of[14], 71), 0)
    image_tokens = draw_image_tokens(jax.random.fold_in(streams_of[14], 71), 0)
    image_offsets = draw_image_offsets(jax.random.fold_in(streams_of[14], 71), 0)
    prefill_gain = jnp.clip(1.0 + 0.18 * jax.random.normal(streams_of[6], (D,), jnp.float32), 0.099609375, 1.8984375).astype(jnp.bfloat16)
    kv_weight = centred(streams_of[7], (D, 2 * HD * KVH), D ** -0.5, 0.0625, ((0, 16), (1, 8)))
    kv_bias = centred(streams_of[8], (2 * HD * KVH,), 1.0, 4.0, ((0, 8),), jnp.float32)
    prompt_lengths = draw_prompt_lengths(jax.random.fold_in(streams_of[14], 71), 0)
    queries = draw_queries(jax.random.fold_in(streams_of[14], 71), 0)
    cache_pages = draw_cache_pages(jax.random.fold_in(streams_of[14], 71), 0)
    page_tables = draw_page_tables(jax.random.fold_in(streams_of[14], 71), 0)
    context_lengths = draw_context_lengths(jax.random.fold_in(streams_of[14], 71), 0)
    return dict(merged_hidden=merged_hidden, merger_weight=merger_weight, merger_bias=merger_bias, text_embed=text_embed, image_tokens=image_tokens, image_offsets=image_offsets, prefill_gain=prefill_gain, kv_weight=kv_weight, kv_bias=kv_bias, prompt_lengths=prompt_lengths, queries=queries, cache_pages=cache_pages, page_tables=page_tables, context_lengths=context_lengths)


EPSILON = 1e-06
THETA = 1000000.0
MASKED = -1e+30

def place_images(text_rows, image_rows, image_counts, image_starts):
    positions = jnp.arange(text_rows.shape[0], dtype=jnp.int32)[:, None]
    earlier = (jnp.cumsum(image_counts) - image_counts).astype(jnp.int32)
    inside_img = (positions >= image_starts[None, :]) & (positions < (image_starts + image_counts)[None, :])
    source_row = lax.optimization_barrier(jnp.sum(jnp.where(inside_img, earlier[None, :] + positions - image_starts[None, :], 0), axis=1)).astype(jnp.int32)
    covered = jnp.any(inside_img, axis=1)
    picked_rows = jnp.take(image_rows, source_row, axis=0)
    return jnp.where(covered[:, None], picked_rows, text_rows)

def rotate_keys(packed, head_dim):
    seq_len = packed.shape[0]
    head_count = packed.shape[1] // (2 * head_dim)
    head_grid = packed.reshape(seq_len, head_count, 2, head_dim)
    key_part = head_grid[:, :, 0, :]
    value_part = head_grid[:, :, 1, :]
    half_dim = head_dim // 2
    frequency = THETA ** (-jnp.arange(half_dim, dtype=jnp.float32) * 2.0 / head_dim)
    angles = jnp.arange(seq_len, dtype=jnp.float32)[:, None] * frequency[None, :]
    cosine = jnp.cos(angles)[:, None, :]
    sine_table = jnp.sin(angles)[:, None, :]
    first_half = key_part[..., :half_dim]
    second_half = key_part[..., half_dim:]
    rotated = jnp.concatenate([first_half * cosine - second_half * sine_table, second_half * cosine + first_half * sine_table], axis=-1)
    return jnp.stack([rotated, value_part], axis=2).reshape(seq_len, head_count * 2 * head_dim).astype(jnp.bfloat16)

def attend(asked, page_pool, page_table, live_lengths, head_dim):
    request_count = asked.shape[0]
    head_count = page_pool.shape[2] // (2 * head_dim)
    per_head = asked.shape[1] // (head_count * head_dim)
    gathered = jnp.take(page_pool, page_table, axis=0)
    context_span = page_table.shape[1] * page_pool.shape[1]
    gathered = gathered.reshape(request_count, context_span, head_count, 2, head_dim)
    key_rows = gathered[:, :, :, 0, :].astype(jnp.float32)
    value_rows = gathered[:, :, :, 1, :].astype(jnp.float32)
    grouped = asked.reshape(request_count, head_count, per_head, head_dim).astype(jnp.float32)
    scores = jnp.einsum('rhgd,rthd->rhgt', grouped, key_rows) / math.sqrt(head_dim)
    live_mask = jnp.arange(context_span, dtype=jnp.int32)[None, :] < live_lengths[:, None]
    scores = jnp.where(live_mask[:, None, None, :], scores, MASKED)
    row_max = lax.optimization_barrier(jnp.max(scores, axis=-1, keepdims=True))
    weights = jnp.exp(scores - row_max)
    weights = (weights / lax.optimization_barrier(jnp.sum(weights, axis=-1, keepdims=True))).astype(jnp.bfloat16)
    mixed = jnp.einsum('rhgt,rthd->rhgd', weights.astype(jnp.float32), value_rows)
    return mixed.reshape(request_count, head_count * per_head * head_dim).astype(jnp.bfloat16)

def reference(merged_hidden, merger_weight, merger_bias, text_embed, image_tokens, image_offsets, prefill_gain, kv_weight, kv_bias, prompt_lengths, queries, cache_pages, page_tables, context_lengths):
    image_rows = (jnp.dot(merged_hidden, merger_weight, preferred_element_type=jnp.float32) + merger_bias).astype(jnp.bfloat16)
    image_blocks = jnp.roll(image_rows.reshape(PROMPTS, MD, D), N_SEQ, axis=0)
    text_blocks = text_embed.reshape(PROMPTS, PL, D)

    def prefill_one(bundle):
        text_rows, image_block, image_counts, image_starts = bundle
        embedded = place_images(text_rows, image_block, image_counts.astype(jnp.int32), image_starts.astype(jnp.int32))
        widened = embedded.astype(jnp.float32)
        scaling = lax.rsqrt(lax.optimization_barrier(jnp.sum(widened * widened, axis=1, keepdims=True)) / D + EPSILON)
        normed = (widened * scaling * prefill_gain.astype(jnp.float32)).astype(jnp.bfloat16)
        projected = jnp.dot(normed, kv_weight, preferred_element_type=jnp.float32) + kv_bias
        return rotate_keys(projected, HD)
    prompt_blocks = lax.map(prefill_one, (text_blocks, image_blocks, image_tokens, image_offsets))
    fresh_blocks = jnp.roll(prompt_blocks, N_SEQ, axis=0).reshape(PROMPTS, MAXP, PAGE, 2 * HD * KVH)
    fresh_lengths = jnp.roll(prompt_lengths, N_SEQ).astype(jnp.int32)
    pool_blocks = cache_pages.reshape(PROMPTS, POOL, PAGE, 2 * HD * KVH)
    table_blocks = page_tables.reshape(PROMPTS, RQ, MAXP)
    length_blocks = context_lengths.reshape(PROMPTS, RQ)
    query_blocks = queries.reshape(PROMPTS, RQ + 1, QH * HD)

    def decode_one(bundle):
        page_pool, fresh_pages, tables, lengths_now, fresh_length, asked = bundle
        combined = jnp.concatenate([page_pool, fresh_pages], axis=0)
        appended = (POOL + jnp.arange(MAXP, dtype=jnp.int32)).astype(jnp.int32)[None, :]
        all_tables = jnp.concatenate([tables.astype(jnp.int32), appended], axis=0)
        all_lengths = jnp.concatenate([lengths_now.astype(jnp.int32), fresh_length.astype(jnp.int32)[None]], axis=0)
        return attend(asked, combined, all_tables, all_lengths, HD)
    decoded = lax.map(decode_one, (pool_blocks, fresh_blocks, table_blocks, length_blocks, fresh_lengths, query_blocks))
    return (prompt_blocks.reshape(PROMPTS * PL, 2 * HD * KVH), decoded.reshape(PROMPTS * (RQ + 1), QH * HD))
```

```python
import math

import jax
import jax.numpy as jnp
from jax import lax
from jax.sharding import PartitionSpec as P

D = 8192
HD = 128


EPSILON = 1e-06
THETA = 1000000.0
MASKED = -1e30


def hop(value, section_steps, seq_steps):
    sections = lax.axis_size("section")
    owners = lax.axis_size("seq")
    pairs = [
        (x * owners + z, (x + section_steps) % sections * owners + (z + seq_steps) % owners)
        for x in range(sections)
        for z in range(owners)
    ]
    return lax.ppermute(value, ("section", "seq"), pairs)


def tp_hop(value, steps):
    count = lax.axis_size("tp")
    return lax.ppermute(value, "tp", [(t, (t + steps) % count) for t in range(count)])


def core_swap(value):
    return lax.ppermute(value, "tp", [(t, t ^ 1) for t in range(lax.axis_size("tp"))])


def merged_images(merged_hidden, merger_weight, merger_bias):
    f32 = jnp.float32
    z = lax.axis_index("seq")
    blocks = merged_hidden.reshape(4, 4, 48, merged_hidden.shape[1])

    def share(step):
        rows = lax.dynamic_index_in_dim(blocks, (z + step) % 4, axis=1, keepdims=False)
        return jnp.dot(
            rows.reshape(192, rows.shape[2]), merger_weight, preferred_element_type=f32
        )

    half = merger_weight.shape[1] // 2
    far = share(2).astype(jnp.bfloat16)
    far_low = hop(far[:, :half], 0, 2)
    far_high = hop(far[:, half:], 0, -2)
    right = hop(share(1).astype(jnp.bfloat16), 0, 1)
    left = hop(share(3).astype(jnp.bfloat16), 0, -1)
    own = share(0)
    total = (
        own
        + right.astype(f32)
        + left.astype(f32)
        + jnp.concatenate([far_low, far_high], axis=1).astype(f32)
    )
    total = total.astype(jnp.bfloat16).reshape(4, 48, total.shape[1])

    def block(step):
        return lax.dynamic_index_in_dim(total, (z // 4 + step) % 4, axis=0, keepdims=False)

    summed = merger_bias
    for step in (2, 1, 3, 0):
        summed = summed + hop(block(step), 1, 4 * step).astype(f32)
    return summed.astype(jnp.bfloat16)


def gathered_text(text_embed, gain):
    t = lax.axis_index("tp")
    y, core = t // 2, t % 2
    rows = text_embed.shape[0]
    sent = jnp.concatenate(
        [text_embed, jnp.broadcast_to(gain[None, :], (16, gain.shape[0]))], axis=0
    )
    mine = jnp.stack([sent, tp_hop(sent, -2), tp_hop(sent, 4), tp_hop(sent, 2)])
    others = core_swap(mine)
    both = jnp.stack([mine, others])
    parts = []
    for k in range(lax.axis_size("tp")):
        part = lax.dynamic_slice(
            both, ((core + k) % 2, (k // 2 - y) % 4, 0, 0), (1, 1) + sent.shape
        )
        parts.append(part.reshape(sent.shape))
    whole = jnp.concatenate(parts, axis=1)
    return whole[:rows], whole[rows]


def normalized(rows, gain):
    widened = rows.astype(jnp.float32)
    squares = jnp.sum(widened * widened, axis=1, keepdims=True)
    scaling = lax.rsqrt(squares / D + EPSILON)
    return (widened * scaling * gain.astype(jnp.float32)).astype(jnp.bfloat16)


def placed(text_rows, image_rows, image_counts, image_starts):
    positions = jnp.arange(text_rows.shape[0], dtype=jnp.int32)[:, None]
    earlier = jnp.cumsum(image_counts) - image_counts
    inside_img = (positions >= image_starts[None, :]) & (
        positions < (image_starts + image_counts)[None, :]
    )
    source_row = jnp.sum(
        jnp.where(inside_img, earlier[None, :] + positions - image_starts[None, :], 0), axis=1
    )
    covered = jnp.any(inside_img, axis=1)
    picked_rows = jnp.take(image_rows, source_row, axis=0)
    return jnp.where(covered[:, None], picked_rows, text_rows)


def rotate_keys(packed, head_dim):
    seq_len = packed.shape[0]
    head_count = packed.shape[1] // (2 * head_dim)
    head_grid = packed.reshape(seq_len, head_count, 2, head_dim)
    key_part = head_grid[:, :, 0, :]
    value_part = head_grid[:, :, 1, :]
    half_dim = head_dim // 2
    frequency = THETA ** (-jnp.arange(half_dim, dtype=jnp.float32) * 2.0 / head_dim)
    angles = jnp.arange(seq_len, dtype=jnp.float32)[:, None] * frequency[None, :]
    cosine = jnp.cos(angles)[:, None, :]
    sine_table = jnp.sin(angles)[:, None, :]
    first_half = key_part[..., :half_dim]
    second_half = key_part[..., half_dim:]
    rotated = jnp.concatenate(
        [
            first_half * cosine - second_half * sine_table,
            second_half * cosine + first_half * sine_table,
        ],
        axis=-1,
    )
    return (
        jnp.stack([rotated, value_part], axis=2)
        .reshape(seq_len, head_count * 2 * head_dim)
        .astype(jnp.bfloat16)
    )


def attend(asked, page_pool, page_table, live_lengths, head_dim):
    request_count = asked.shape[0]
    head_count = page_pool.shape[2] // (2 * head_dim)
    per_head = asked.shape[1] // (head_count * head_dim)
    gathered = jnp.take(page_pool, page_table, axis=0)
    context_span = page_table.shape[1] * page_pool.shape[1]
    gathered = gathered.reshape(request_count, context_span, head_count, 2, head_dim)
    key_rows = gathered[:, :, :, 0, :]
    value_rows = gathered[:, :, :, 1, :]
    grouped = asked.reshape(request_count, head_count, per_head, head_dim)
    scores = jnp.einsum(
        "rhgd,rthd->rhgt", grouped, key_rows, preferred_element_type=jnp.float32
    ) / math.sqrt(head_dim)
    live_mask = jnp.arange(context_span, dtype=jnp.int32)[None, :] < live_lengths[:, None]
    scores = jnp.where(live_mask[:, None, None, :], scores, MASKED)
    row_max = jnp.max(scores, axis=-1, keepdims=True)
    weights = jnp.exp(scores - row_max)
    weights = (weights / jnp.sum(weights, axis=-1, keepdims=True)).astype(jnp.bfloat16)
    mixed = jnp.einsum("rhgt,rthd->rhgd", weights, value_rows, preferred_element_type=jnp.float32)
    return mixed.reshape(request_count, head_count * per_head * head_dim).astype(jnp.bfloat16)


def attend_fresh(asked, prompt_cache, length, head_dim):
    keys = prompt_cache[:, :head_dim]
    values = prompt_cache[:, head_dim:]
    scores = jnp.einsum("gd,td->gt", asked, keys, preferred_element_type=jnp.float32)
    scores = scores / math.sqrt(head_dim)
    live = jnp.arange(keys.shape[0], dtype=jnp.int32)[None, :] < length
    scores = jnp.where(live, scores, MASKED)
    weights = jnp.exp(scores - jnp.max(scores, axis=-1, keepdims=True))
    weights = (weights / jnp.sum(weights, axis=-1, keepdims=True)).astype(jnp.bfloat16)
    mixed = jnp.einsum("gt,td->gd", weights, values, preferred_element_type=jnp.float32)
    return mixed.astype(jnp.bfloat16)


def per_device(
    merged_hidden,
    merger_weight,
    merger_bias,
    text_embed,
    image_tokens,
    image_offsets,
    prefill_gain,
    kv_weight,
    kv_bias,
    prompt_lengths,
    queries,
    cache_pages,
    page_tables,
    context_lengths,
):
    weight = lax.all_gather(kv_weight, "seq", axis=0, tiled=True)
    image_rows = merged_images(merged_hidden, merger_weight, merger_bias)
    text_all, gain_all = gathered_text(text_embed, prefill_gain)
    resident = queries.shape[0] - 1
    asked = hop(queries[resident:], -1, 0)
    resident_out = attend(queries[:resident], cache_pages, page_tables, context_lengths, HD)
    text_normed = normalized(text_all, gain_all)
    image_normed = normalized(lax.all_gather(image_rows, "tp", axis=1, tiled=True), gain_all)
    text_projected = jnp.dot(text_normed, weight, preferred_element_type=jnp.float32)
    image_projected = jnp.dot(image_normed, weight, preferred_element_type=jnp.float32)
    projected = placed(text_projected, image_projected, image_tokens[0], image_offsets[0])
    prompt_cache = rotate_keys(projected + kv_bias, HD)
    place = lax.axis_index("section") * lax.axis_size("seq") + lax.axis_index("seq")
    length = lax.dynamic_slice_in_dim(prompt_lengths, place, 1, 0)[0]
    fresh = attend_fresh(asked.reshape(-1, HD), prompt_cache, length, HD)
    fresh_out = hop(fresh.reshape(1, -1), 1, 0)
    decode_out = jnp.concatenate([resident_out, fresh_out], axis=0)
    return (prompt_cache, decode_out)


def solution(mesh):
    return jax.shard_map(
        per_device,
        mesh=mesh,
        in_specs=(
            P("section", "seq"),
            P("seq", "tp"),
            P("tp"),
            P(("section", "seq"), "tp"),
            P(("section", "seq"), None),
            P(("section", "seq"), None),
            P("tp"),
            P("seq", "tp"),
            P("tp"),
            P(),
            P(("section", "seq"), "tp"),
            P(("section", "seq"), None, "tp"),
            P(("section", "seq"), None),
            P(("section", "seq")),
        ),
        out_specs=(P(("section", "seq"), "tp"), P(("section", "seq"), "tp")),
        check_vma=False,
    )
```

```python
import math

import jax
import jax.numpy as jnp
from jax import lax
from jax.experimental import pallas as pl
from jax.experimental.pallas import tpu as pltpu
from jax.sharding import PartitionSpec as P

D = 8192
TP = ("row", "core")
HD = 128
EPSILON = 1e-06
THETA = 1000000.0
MASKED = -1e30
F32 = jnp.float32
BF16 = jnp.bfloat16
SMALL = pl.CostEstimate(flops=1024, bytes_accessed=1024, transcendentals=0)
VMEM_BYTES = 32 * 1024 * 1024


def whole(memory_space=pltpu.VMEM):
    return pl.BlockSpec(memory_space=memory_space)


def hop(value, section_steps, seq_steps):
    sections = lax.axis_size("section")
    owners = lax.axis_size("seq")
    pairs = [
        (x * owners + z, (x + section_steps) % sections * owners + (z + seq_steps) % owners)
        for x in range(sections)
        for z in range(owners)
    ]
    return lax.ppermute(value, ("section", "seq"), pairs)


def after(value, *others):
    return lax.optimization_barrier((value,) + others)[0]


def wide(value):
    return value.astype(F32)


def shares_kernel(
    place_ref, hidden_ref, weight_ref, text_ref, gain_ref,
    far_ref, other_ref, near_ref, own_ref, sent_ref,
):
    weight = weight_ref[...]
    for step, out_ref in ((2, far_ref), (1, other_ref), (3, near_ref), (0, own_ref)):
        quarter = lax.rem(place_ref[0] + step, 4)
        for k in range(4):
            start = pl.multiple_of((4 * k + quarter) * 48, 16)
            out = jnp.dot(hidden_ref[pl.ds(start, 48), :], weight, preferred_element_type=F32)
            out_ref[pl.ds(48 * k, 48), :] = out.astype(out_ref.dtype)
    rows = text_ref.shape[0]
    gain = jnp.broadcast_to(wide(gain_ref[...]), (16, gain_ref.shape[1])).astype(BF16)
    for k in range(sent_ref.shape[0]):
        sent_ref[k, :rows, :] = text_ref[...]
        sent_ref[k, rows:, :] = gain


def merger_shares(merged_hidden, merger_weight, text_embed, gain):
    shape = (192, merger_weight.shape[1])
    rows, width = text_embed.shape
    shapes = [jax.ShapeDtypeStruct(shape, kind) for kind in (BF16, BF16, F32, F32)]
    shapes.append(jax.ShapeDtypeStruct((lax.axis_size("row"), rows + 16, width), BF16))
    return pl.pallas_call(
        shares_kernel,
        out_shape=tuple(shapes),
        in_specs=[whole(pltpu.SMEM)] + [whole()] * 4,
        out_specs=(whole(),) * 5,
        cost_estimate=SMALL,
        compiler_params=pltpu.CompilerParams(vmem_limit_bytes=VMEM_BYTES),
        name="merger_shares",
    )(lax.axis_index("seq")[None], merged_hidden, merger_weight, text_embed, gain[None, :])


def summed_images(shares, merger_bias, text, queries):
    z = lax.axis_index("seq")
    far, other, near, own = shares
    far = hop(far, 0, -1)
    other = hop(other, 0, 1)
    near = hop((near + wide(far)).astype(BF16), 0, -1)
    total = (own + wide(other) + wide(near)).reshape(4, 48, own.shape[1])
    total, text = lax.optimization_barrier((total, text))
    others = lax.ppermute(text, "core", [(0, 1), (1, 0)])

    def block(step):
        return lax.dynamic_index_in_dim(total, (z // 4 + step) % 4, axis=0, keepdims=False)

    far = hop(block(2).astype(BF16), 0, -4)
    other = hop(block(1).astype(BF16), 1, 4)
    own = hop((block(0) + merger_bias).astype(BF16), 1, 0)
    near = (wide(block(3)) + wide(far)).astype(BF16)
    near, text, others, queries = lax.optimization_barrier((near, text, others, queries))
    near = hop(near, 1, -4)
    return (wide(own) + wide(other) + wide(near)).astype(BF16), text, others, queries


def text_kernel(core_ref, mine_ref, others_ref, out_ref, gain_ref):
    rows = out_ref.shape[0]
    pieces, width = mine_ref.shape[0], mine_ref.shape[2]
    core = core_ref[0]
    sides = ((mine_ref, core), (others_ref, 1 - core))
    squares = jnp.zeros((rows, 1), F32)
    for ref, side in sides:
        for k in range(pieces):
            part = wide(ref[k, :rows, :])
            squares = squares + jnp.sum(part * part, axis=1, keepdims=True)
    scaling = lax.rsqrt(squares / D + EPSILON)
    for ref, side in sides:
        for k in range(pieces):
            columns = pl.ds(pl.multiple_of((2 * k + side) * width, width), width)
            gain = wide(ref[k, rows:, :])
            gain_ref[:, columns] = gain
            out_ref[:, columns] = (wide(ref[k, :rows, :]) * scaling * gain[:1]).astype(BF16)


def normed_text(mine, others):
    rows = mine.shape[1] - 16
    return pl.pallas_call(
        text_kernel,
        out_shape=(
            jax.ShapeDtypeStruct((rows, D), BF16),
            jax.ShapeDtypeStruct((16, D), F32),
        ),
        in_specs=[whole(pltpu.SMEM), whole(), whole()],
        out_specs=(whole(), whole()),
        cost_estimate=pl.CostEstimate(
            flops=20 * 1024 * 1024, bytes_accessed=9 * 1024 * 1024, transcendentals=0
        ),
        compiler_params=pltpu.CompilerParams(vmem_limit_bytes=VMEM_BYTES),
        name="text_norm",
    )(lax.axis_index("core")[None], mine, others)


def soft(scores, live):
    scores = jnp.where(live, scores / math.sqrt(HD), MASKED)
    weights = jnp.exp(scores - jnp.max(scores, axis=-1, keepdims=True))
    return (weights / jnp.sum(weights, axis=-1, keepdims=True)).astype(BF16)


def project_kernel(
    length_ref, counts_ref, starts_ref, image_ref, gain_ref, bias_ref, cos_ref,
    sin_ref, asked_ref, text_ref, weight_ref, cache_ref, fresh_ref,
    rows_ref, rows_arrived_ref, held_ref, arrived_ref,
):
    chunks, depth = held_ref.shape[0], held_ref.shape[1]
    copies = []
    for k in range(chunks):
        part = pl.ds(k * depth, depth)
        copies.append((
            pltpu.make_async_copy(text_ref.at[:, part], rows_ref.at[k], rows_arrived_ref.at[k]),
            pltpu.make_async_copy(weight_ref.at[part, :], held_ref.at[k], arrived_ref.at[k]),
        ))
    for of_text, of_weight in copies:
        of_text.start()
        of_weight.start()
    rows = cache_ref.shape[0]
    images = image_ref.shape[0]
    widened = wide(image_ref[...])
    scaling = lax.rsqrt(jnp.sum(widened * widened, axis=1, keepdims=True) / D + EPSILON)
    position = lax.broadcasted_iota(jnp.int32, (rows, images), 0)
    source = lax.broadcasted_iota(jnp.int32, (rows, images), 1)
    picks = jnp.zeros((rows, images), F32)
    earlier = jnp.int32(0)
    for k in range(4):
        start, count = starts_ref[k], counts_ref[k]
        inside = (position >= start) & (position < start + count)
        chosen = inside & (source == position - start + earlier)
        picks = picks + jnp.where(chosen, 1.0, 0.0)
        earlier = earlier + count
    covered = jnp.sum(picks, axis=1, keepdims=True) > 0.5
    picks = picks.astype(BF16)
    text_total = jnp.zeros((rows, cache_ref.shape[1]), F32)
    image_total = jnp.zeros((images, cache_ref.shape[1]), F32)
    for k, (of_text, of_weight) in enumerate(copies):
        of_text.wait()
        of_weight.wait()
        for first in range(0, depth, 256):
            columns = slice(k * depth + first, k * depth + first + 256)
            weight = held_ref[k, first : first + 256, :]
            normed = wide(image_ref[:, columns]) * scaling * gain_ref[:1, columns]
            text_total = text_total + jnp.dot(
                rows_ref[k, :, first : first + 256], weight, preferred_element_type=F32
            )
            image_total = image_total + jnp.dot(
                normed.astype(BF16), weight, preferred_element_type=F32
            )
    high = image_total.astype(BF16)
    rest = image_total - wide(high)
    middle = rest.astype(BF16)
    low = (rest - wide(middle)).astype(BF16)
    picked = jnp.dot(picks, high, preferred_element_type=F32)
    picked = picked + jnp.dot(picks, middle, preferred_element_type=F32)
    picked = picked + jnp.dot(picks, low, preferred_element_type=F32)
    projected = jnp.where(covered, picked, text_total) + bias_ref[...]
    keys = projected[:, :HD]
    turned = pltpu.roll(keys, HD // 2, axis=1)
    keys = (keys * cos_ref[...] + turned * sin_ref[...]).astype(BF16)
    values = projected[:, HD:].astype(BF16)
    cache_ref[:, :HD] = keys
    cache_ref[:, HD:] = values
    scores = lax.dot_general(
        asked_ref[...], keys, (((1,), (1,)), ((), ())), preferred_element_type=F32
    )
    live = lax.broadcasted_iota(jnp.int32, scores.shape, 1) < length_ref[0]
    mixed = jnp.dot(soft(scores, live), values, preferred_element_type=F32)
    fresh_ref[...] = mixed.astype(BF16)


def project(counts, starts, text, images, gain, weight, bias, asked, length):
    positions = text.shape[0]
    half = HD // 2
    frequency = THETA ** (-jnp.arange(half, dtype=F32) * 2.0 / HD)
    angles = jnp.arange(positions, dtype=F32)[:, None] * frequency[None, :]
    cosine, sine = jnp.cos(angles), jnp.sin(angles)
    cosine = jnp.concatenate([cosine, cosine], axis=1)
    sine = jnp.concatenate([-sine, sine], axis=1)
    chunks = 8
    columns = weight.shape[1]
    return pl.pallas_call(
        project_kernel,
        out_shape=(
            jax.ShapeDtypeStruct((positions, columns), BF16),
            jax.ShapeDtypeStruct(asked.shape, BF16),
        ),
        in_specs=[whole(pltpu.SMEM)] * 3 + [whole()] * 6 + [whole(pl.ANY)] * 2,
        out_specs=(whole(), whole()),
        scratch_shapes=[
            pltpu.VMEM((chunks, positions, D // chunks), BF16),
            pltpu.SemaphoreType.DMA((chunks,)),
            pltpu.VMEM((chunks, D // chunks, columns), BF16),
            pltpu.SemaphoreType.DMA((chunks,)),
        ],
        cost_estimate=SMALL,
        compiler_params=pltpu.CompilerParams(vmem_limit_bytes=60 * 1024 * 1024),
        name="project",
    )(length, counts, starts, images, gain, bias[None, :], cosine, sine, asked, text, weight)


def resident_kernel(tables_ref, lengths_ref, asked_ref, pages_ref, out_ref, scores_ref, mixed_ref):
    requests, pages = tables_ref.shape
    span = scores_ref.shape[1]
    positions = lax.broadcasted_iota(jnp.int32, (8, span), 1)

    def side(request, first):
        return jnp.concatenate(
            [
                pages_ref[tables_ref[request, k], :, first : first + HD]
                for k in range(pages)
            ],
            axis=0,
        )

    scores_ref[requests * 8 :, :] = jnp.zeros((8, span), F32)
    mixed_ref[requests * 8 :, :] = jnp.zeros((8, HD), F32)
    for request in range(requests):
        rows = pl.ds(request * 8, 8)
        scores = lax.dot_general(
            asked_ref[rows, :].astype(BF16),
            side(request, 0),
            (((1,), (1,)), ((), ())),
            preferred_element_type=F32,
        )
        scores_ref[rows, :] = jnp.where(
            positions < lengths_ref[request], scores / math.sqrt(HD), MASKED
        )
    scores = scores_ref[...]
    weights = jnp.exp(scores - jnp.max(scores, axis=-1, keepdims=True))
    scores_ref[...] = weights / jnp.sum(weights, axis=-1, keepdims=True)
    for request in range(requests):
        rows = pl.ds(request * 8, 8)
        mixed_ref[rows, :] = jnp.dot(
            scores_ref[rows, :].astype(BF16), side(request, HD), preferred_element_type=F32
        )
    out_ref[...] = mixed_ref[...].astype(BF16)


def attend_resident(queries, cache_pages, page_tables, context_lengths):
    heads = queries.size // HD
    span = page_tables.shape[1] * cache_pages.shape[1]
    out = pl.pallas_call(
        resident_kernel,
        out_shape=jax.ShapeDtypeStruct((heads, HD), BF16),
        in_specs=[whole(pltpu.SMEM), whole(pltpu.SMEM), whole(), whole()],
        out_specs=whole(),
        scratch_shapes=[pltpu.VMEM((heads, span), F32), pltpu.VMEM((heads, HD), F32)],
        cost_estimate=SMALL,
        compiler_params=pltpu.CompilerParams(vmem_limit_bytes=VMEM_BYTES),
        name="resident",
    )(page_tables, context_lengths, wide(queries).reshape(heads, HD), cache_pages)
    return out


def per_device(
    merged_hidden,
    merger_weight,
    merger_bias,
    text_embed,
    image_tokens,
    image_offsets,
    prefill_gain,
    kv_weight,
    kv_bias,
    prompt_lengths,
    queries,
    cache_pages,
    page_tables,
    context_lengths,
):
    weight = lax.all_gather(kv_weight, "seq", axis=0, tiled=True)
    *shares, text = merger_shares(merged_hidden, merger_weight, text_embed, prefill_gain)
    text = lax.all_to_all(text, "row", 0, 0, tiled=True)
    image_rows, text, others, queries = summed_images(shares, merger_bias, text, queries)
    text_normed, gain_all = normed_text(text, others)
    image_all = lax.all_gather(image_rows, TP, axis=1, tiled=True)
    resident = queries.shape[0] - 1
    asked = hop(queries[resident:].reshape(-1, HD), -1, 0)
    resident_out = attend_resident(queries, cache_pages, page_tables, context_lengths)
    place = lax.axis_index("section") * lax.axis_size("seq") + lax.axis_index("seq")
    length = lax.dynamic_slice_in_dim(prompt_lengths, place, 1, 0)
    prompt_cache, fresh = project(
        image_tokens[0], image_offsets[0], text_normed, image_all, gain_all, weight, kv_bias,
        asked, length,
    )
    fresh_out = hop(fresh, 1, 0).reshape(1, -1)
    last = jnp.arange(resident + 1, dtype=jnp.int32)[:, None] == resident
    decode_out = jnp.where(last, fresh_out, resident_out.reshape(queries.shape))
    return (prompt_cache, decode_out)


def solution(mesh):
    sections, owners, columns = mesh.devices.shape
    devices = mesh.devices.reshape(sections, owners, columns // 2, 2)
    mesh = jax.sharding.Mesh(devices, ("section", "seq") + TP)
    return jax.shard_map(
        per_device,
        mesh=mesh,
        in_specs=(
            P("section", "seq"),
            P("seq", TP),
            P(TP),
            P(("section", "seq"), TP),
            P(("section", "seq"), None),
            P(("section", "seq"), None),
            P(TP),
            P("seq", TP),
            P(TP),
            P(),
            P(("section", "seq"), TP),
            P(("section", "seq"), None, TP),
            P(("section", "seq"), None),
            P(("section", "seq")),
        ),
        out_specs=(P(("section", "seq"), TP), P(("section", "seq"), TP)),
        check_vma=False,
    )
```

```python
import math

import jax
import jax.numpy as jnp
from jax import lax
from jax.experimental import pallas as pl
from jax.experimental.pallas import tpu as pltpu
from jax.sharding import PartitionSpec as P

D = 8192
TP = ("row", "core")
HD = 128
EPSILON = 1e-06
THETA = 1000000.0
MASKED = -1e30
F32 = jnp.float32
BF16 = jnp.bfloat16
SMALL = pl.CostEstimate(flops=1024, bytes_accessed=1024, transcendentals=0)
VMEM_BYTES = 32 * 1024 * 1024


def whole(memory_space=pltpu.VMEM):
    return pl.BlockSpec(memory_space=memory_space)


def hop(value, section_steps, seq_steps):
    sections = lax.axis_size("section")
    owners = lax.axis_size("seq")
    pairs = [
        (x * owners + z, (x + section_steps) % sections * owners + (z + seq_steps) % owners)
        for x in range(sections)
        for z in range(owners)
    ]
    return lax.ppermute(value, ("section", "seq"), pairs)


def after(value, *others):
    return lax.optimization_barrier((value,) + others)[0]


def wide(value):
    return value.astype(F32)


def shares_kernel(
    place_ref, hidden_ref, weight_ref, text_ref, gain_ref,
    far_ref, other_ref, near_ref, own_ref, sent_ref,
):
    weight = weight_ref[...]
    for step, out_ref in ((2, far_ref), (1, other_ref), (3, near_ref), (0, own_ref)):
        quarter = lax.rem(place_ref[0] + step, 4)
        for k in range(4):
            start = pl.multiple_of((4 * k + quarter) * 48, 16)
            out = jnp.dot(hidden_ref[pl.ds(start, 48), :], weight, preferred_element_type=F32)
            out_ref[pl.ds(48 * k, 48), :] = out.astype(out_ref.dtype)
    rows = text_ref.shape[0]
    gain = jnp.broadcast_to(wide(gain_ref[...]), (16, gain_ref.shape[1])).astype(BF16)
    for k in range(sent_ref.shape[0]):
        sent_ref[k, :rows, :] = text_ref[...]
        sent_ref[k, rows:, :] = gain


def merger_shares(merged_hidden, merger_weight, text_embed, gain):
    shape = (192, merger_weight.shape[1])
    rows, width = text_embed.shape
    shapes = [jax.ShapeDtypeStruct(shape, kind) for kind in (BF16, BF16, F32, F32)]
    shapes.append(jax.ShapeDtypeStruct((lax.axis_size("row"), rows + 16, width), BF16))
    return pl.pallas_call(
        shares_kernel,
        out_shape=tuple(shapes),
        in_specs=[whole(pltpu.SMEM)] + [whole()] * 4,
        out_specs=(whole(),) * 5,
        cost_estimate=SMALL,
        compiler_params=pltpu.CompilerParams(vmem_limit_bytes=VMEM_BYTES),
        name="merger_shares",
    )(lax.axis_index("seq")[None], merged_hidden, merger_weight, text_embed, gain[None, :])


def summed_images(shares, merger_bias, text, queries):
    z = lax.axis_index("seq")
    far, other, near, own = shares
    far = hop(far, 0, -1)
    other = hop(other, 0, 1)
    near = hop((near + wide(far)).astype(BF16), 0, -1)
    total = (own + wide(other) + wide(near)).reshape(4, 48, own.shape[1])
    total, text = lax.optimization_barrier((total, text))
    text = lax.all_to_all(text, "row", 0, 0, tiled=True)

    def block(step):
        return lax.dynamic_index_in_dim(total, (z // 4 + step) % 4, axis=0, keepdims=False)

    far = hop(block(2).astype(BF16), 0, -4)
    other = hop(block(1).astype(BF16), 1, 4)
    own = hop((block(0) + merger_bias).astype(BF16), 1, 0)
    near = (wide(block(3)) + wide(far)).astype(BF16)
    queries = after(queries, near)
    near = hop(near, 1, -4)
    rows = (wide(own) + wide(other) + wide(near)).astype(BF16)
    rows, text = lax.optimization_barrier((rows, text))
    others = lax.ppermute(text, "core", [(0, 1), (1, 0)])
    return rows, text, others, queries


def soft(scores, live):
    scores = jnp.where(live, scores / math.sqrt(HD), MASKED)
    weights = jnp.exp(scores - jnp.max(scores, axis=-1, keepdims=True))
    return (weights / jnp.sum(weights, axis=-1, keepdims=True)).astype(BF16)


def project_kernel(
    length_ref, core_ref, counts_ref, starts_ref, mine_ref, others_ref, image_ref, bias_ref,
    cos_ref, sin_ref, asked_ref, weight_ref, cache_ref, fresh_ref, held_ref, arrived_ref,
):
    chunks, depth = held_ref.shape[0], held_ref.shape[1]
    copies = [
        pltpu.make_async_copy(
            weight_ref.at[pl.ds(k * depth, depth), :], held_ref.at[k], arrived_ref.at[k]
        )
        for k in range(chunks)
    ]
    for copy in copies:
        copy.start()
    rows = cache_ref.shape[0]
    images = image_ref.shape[0]
    widened = wide(image_ref[...])
    scaling = lax.rsqrt(jnp.sum(widened * widened, axis=1, keepdims=True) / D + EPSILON)
    position = lax.broadcasted_iota(jnp.int32, (rows, images), 0)
    source = lax.broadcasted_iota(jnp.int32, (rows, images), 1)
    picks = jnp.zeros((rows, images), F32)
    earlier = jnp.int32(0)
    for k in range(4):
        start, count = starts_ref[k], counts_ref[k]
        inside = (position >= start) & (position < start + count)
        chosen = inside & (source == position - start + earlier)
        picks = picks + jnp.where(chosen, 1.0, 0.0)
        earlier = earlier + count
    covered = jnp.sum(picks, axis=1, keepdims=True) > 0.5
    picks = picks.astype(BF16)
    core = core_ref[0]
    sides = ((mine_ref, core), (others_ref, 1 - core))
    squares = jnp.zeros((rows, 1), F32)
    for ref, side in sides:
        for row in range(chunks // 2):
            part = wide(ref[row, :rows, :])
            squares = squares + jnp.sum(part * part, axis=1, keepdims=True)
    text_scaling = lax.rsqrt(squares / D + EPSILON)
    text_total = jnp.zeros((rows, cache_ref.shape[1]), F32)
    image_total = jnp.zeros((images, cache_ref.shape[1]), F32)
    for row in range(chunks // 2):
        copies[2 * row].wait()
        copies[2 * row + 1].wait()
        for ref, side in sides:
            chunk = 2 * row + side
            for first in range(0, depth, 256):
                part = slice(first, first + 256)
                columns = pl.ds(pl.multiple_of(chunk * depth + first, 256), 256)
                gain = wide(ref[row, rows:, part])[:1]
                weight = held_ref[chunk, part, :]
                normed = wide(ref[row, :rows, part]) * text_scaling * gain
                text_total = text_total + jnp.dot(
                    normed.astype(BF16), weight, preferred_element_type=F32
                )
                normed = wide(image_ref[:, columns]) * scaling * gain
                image_total = image_total + jnp.dot(
                    normed.astype(BF16), weight, preferred_element_type=F32
                )
    high = image_total.astype(BF16)
    rest = image_total - wide(high)
    middle = rest.astype(BF16)
    low = (rest - wide(middle)).astype(BF16)
    picked = jnp.dot(picks, high, preferred_element_type=F32)
    picked = picked + jnp.dot(picks, middle, preferred_element_type=F32)
    picked = picked + jnp.dot(picks, low, preferred_element_type=F32)
    projected = jnp.where(covered, picked, text_total) + bias_ref[...]
    keys = projected[:, :HD]
    turned = pltpu.roll(keys, HD // 2, axis=1)
    keys = (keys * cos_ref[...] + turned * sin_ref[...]).astype(BF16)
    values = projected[:, HD:].astype(BF16)
    cache_ref[:, :HD] = keys
    cache_ref[:, HD:] = values
    scores = lax.dot_general(
        asked_ref[...], keys, (((1,), (1,)), ((), ())), preferred_element_type=F32
    )
    live = lax.broadcasted_iota(jnp.int32, scores.shape, 1) < length_ref[0]
    mixed = jnp.dot(soft(scores, live), values, preferred_element_type=F32)
    fresh_ref[...] = mixed.astype(BF16)


def project(counts, starts, mine, others, images, weight, bias, asked, length):
    positions = mine.shape[1] - 16
    half = HD // 2
    frequency = THETA ** (-jnp.arange(half, dtype=F32) * 2.0 / HD)
    angles = jnp.arange(positions, dtype=F32)[:, None] * frequency[None, :]
    cosine, sine = jnp.cos(angles), jnp.sin(angles)
    cosine = jnp.concatenate([cosine, cosine], axis=1)
    sine = jnp.concatenate([-sine, sine], axis=1)
    chunks = 8
    columns = weight.shape[1]
    return pl.pallas_call(
        project_kernel,
        out_shape=(
            jax.ShapeDtypeStruct((positions, columns), BF16),
            jax.ShapeDtypeStruct(asked.shape, BF16),
        ),
        in_specs=[whole(pltpu.SMEM)] * 4 + [whole()] * 7 + [whole(pl.ANY)],
        out_specs=(whole(), whole()),
        scratch_shapes=[
            pltpu.VMEM((chunks, D // chunks, columns), BF16),
            pltpu.SemaphoreType.DMA((chunks,)),
        ],
        cost_estimate=SMALL,
        compiler_params=pltpu.CompilerParams(vmem_limit_bytes=VMEM_BYTES),
        name="project",
    )(
        length, lax.axis_index("core")[None], counts, starts, mine, others, images,
        bias[None, :], cosine, sine, asked, weight,
    )


def resident_kernel(tables_ref, lengths_ref, asked_ref, pages_ref, out_ref, scores_ref, mixed_ref):
    requests, pages = tables_ref.shape
    span = scores_ref.shape[1]
    positions = lax.broadcasted_iota(jnp.int32, (8, span), 1)

    def side(request, first):
        return jnp.concatenate(
            [
                pages_ref[tables_ref[request, k], :, first : first + HD]
                for k in range(pages)
            ],
            axis=0,
        )

    scores_ref[requests * 8 :, :] = jnp.zeros((8, span), F32)
    mixed_ref[requests * 8 :, :] = jnp.zeros((8, HD), F32)
    for request in range(requests):
        rows = pl.ds(request * 8, 8)
        scores = lax.dot_general(
            asked_ref[rows, :].astype(BF16),
            side(request, 0),
            (((1,), (1,)), ((), ())),
            preferred_element_type=F32,
        )
        scores_ref[rows, :] = jnp.where(
            positions < lengths_ref[request], scores / math.sqrt(HD), MASKED
        )
    scores = scores_ref[...]
    weights = jnp.exp(scores - jnp.max(scores, axis=-1, keepdims=True))
    scores_ref[...] = weights / jnp.sum(weights, axis=-1, keepdims=True)
    for request in range(requests):
        rows = pl.ds(request * 8, 8)
        mixed_ref[rows, :] = jnp.dot(
            scores_ref[rows, :].astype(BF16), side(request, HD), preferred_element_type=F32
        )
    out_ref[...] = mixed_ref[...].astype(BF16)


def attend_resident(queries, cache_pages, page_tables, context_lengths):
    heads = queries.size // HD
    span = page_tables.shape[1] * cache_pages.shape[1]
    out = pl.pallas_call(
        resident_kernel,
        out_shape=jax.ShapeDtypeStruct((heads, HD), BF16),
        in_specs=[whole(pltpu.SMEM), whole(pltpu.SMEM), whole(), whole()],
        out_specs=whole(),
        scratch_shapes=[pltpu.VMEM((heads, span), F32), pltpu.VMEM((heads, HD), F32)],
        cost_estimate=SMALL,
        compiler_params=pltpu.CompilerParams(vmem_limit_bytes=VMEM_BYTES),
        name="resident",
    )(page_tables, context_lengths, wide(queries).reshape(heads, HD), cache_pages)
    return out


def per_device(
    merged_hidden,
    merger_weight,
    merger_bias,
    text_embed,
    image_tokens,
    image_offsets,
    prefill_gain,
    kv_weight,
    kv_bias,
    prompt_lengths,
    queries,
    cache_pages,
    page_tables,
    context_lengths,
):
    weight = lax.all_gather(kv_weight, "seq", axis=0, tiled=True)
    *shares, text = merger_shares(merged_hidden, merger_weight, text_embed, prefill_gain)
    image_rows, text, others, queries = summed_images(shares, merger_bias, text, queries)
    image_all = lax.all_gather(image_rows, TP, axis=1, tiled=True)
    resident = queries.shape[0] - 1
    asked = hop(queries[resident:].reshape(-1, HD), -1, 0)
    resident_out = attend_resident(queries, cache_pages, page_tables, context_lengths)
    place = lax.axis_index("section") * lax.axis_size("seq") + lax.axis_index("seq")
    length = lax.dynamic_slice_in_dim(prompt_lengths, place, 1, 0)
    prompt_cache, fresh = project(
        image_tokens[0], image_offsets[0], text, others, image_all, weight, kv_bias, asked, length
    )
    fresh_out = hop(fresh, 1, 0).reshape(1, -1)
    last = jnp.arange(resident + 1, dtype=jnp.int32)[:, None] == resident
    decode_out = jnp.where(last, fresh_out, resident_out.reshape(queries.shape))
    return (prompt_cache, decode_out)


def solution(mesh):
    sections, owners, columns = mesh.devices.shape
    devices = mesh.devices.reshape(sections, owners, columns // 2, 2)
    mesh = jax.sharding.Mesh(devices, ("section", "seq") + TP)
    return jax.shard_map(
        per_device,
        mesh=mesh,
        in_specs=(
            P("section", "seq"),
            P("seq", TP),
            P(TP),
            P(("section", "seq"), TP),
            P(("section", "seq"), None),
            P(("section", "seq"), None),
            P(TP),
            P("seq", TP),
            P(TP),
            P(),
            P(("section", "seq"), TP),
            P(("section", "seq"), None, TP),
            P(("section", "seq"), None),
            P(("section", "seq")),
        ),
        out_specs=(P(("section", "seq"), TP), P(("section", "seq"), TP)),
        check_vma=False,
    )
```

```python
import math

import jax
import jax.numpy as jnp
from jax import lax
from jax.experimental import pallas as pl
from jax.experimental.pallas import tpu as pltpu
from jax.sharding import PartitionSpec as P

D = 8192
TP = ("row", "core")
HD = 128
EPSILON = 1e-06
THETA = 1000000.0
MASKED = -1e30
F32 = jnp.float32
BF16 = jnp.bfloat16
SMALL = pl.CostEstimate(flops=1024, bytes_accessed=1024, transcendentals=0)
VMEM_BYTES = 32 * 1024 * 1024


def whole(memory_space=pltpu.VMEM):
    return pl.BlockSpec(memory_space=memory_space)


def hop(value, section_steps, seq_steps):
    sections = lax.axis_size("section")
    owners = lax.axis_size("seq")
    pairs = [
        (x * owners + z, (x + section_steps) % sections * owners + (z + seq_steps) % owners)
        for x in range(sections)
        for z in range(owners)
    ]
    return lax.ppermute(value, ("section", "seq"), pairs)


def after(value, *others):
    return lax.optimization_barrier((value,) + others)[0]


def wide(value):
    return value.astype(F32)


def shares_kernel(
    place_ref, hidden_ref, weight_ref, text_ref, gain_ref,
    far_ref, other_ref, near_ref, own_ref, sent_ref,
):
    weight = weight_ref[...]
    for step, out_ref in ((2, far_ref), (1, other_ref), (3, near_ref), (0, own_ref)):
        quarter = lax.rem(place_ref[0] + step, 4)
        for k in range(4):
            start = pl.multiple_of((4 * k + quarter) * 48, 16)
            out = jnp.dot(hidden_ref[pl.ds(start, 48), :], weight, preferred_element_type=F32)
            out_ref[pl.ds(48 * k, 48), :] = out.astype(out_ref.dtype)
    rows = text_ref.shape[0]
    gain = jnp.broadcast_to(wide(gain_ref[...]), (16, gain_ref.shape[1])).astype(BF16)
    for k in range(sent_ref.shape[0]):
        sent_ref[k, :rows, :] = text_ref[...]
        sent_ref[k, rows:, :] = gain


def merger_shares(merged_hidden, merger_weight, text_embed, gain):
    shape = (192, merger_weight.shape[1])
    rows, width = text_embed.shape
    shapes = [jax.ShapeDtypeStruct(shape, kind) for kind in (BF16, BF16, F32, F32)]
    shapes.append(jax.ShapeDtypeStruct((lax.axis_size("row"), rows + 16, width), BF16))
    return pl.pallas_call(
        shares_kernel,
        out_shape=tuple(shapes),
        in_specs=[whole(pltpu.SMEM)] + [whole()] * 4,
        out_specs=(whole(),) * 5,
        cost_estimate=SMALL,
        compiler_params=pltpu.CompilerParams(vmem_limit_bytes=VMEM_BYTES),
        name="merger_shares",
    )(lax.axis_index("seq")[None], merged_hidden, merger_weight, text_embed, gain[None, :])


def summed_images(shares, merger_bias, text, asked):
    z = lax.axis_index("seq")
    far, other, near, own = shares
    far = hop(far, 0, -1)
    other = hop(other, 0, 1)
    near = hop((near + wide(far)).astype(BF16), 0, -1)
    total = (own + wide(other) + wide(near)).reshape(4, 48, own.shape[1])
    total, text = lax.optimization_barrier((total, text))
    text = lax.all_to_all(text, "row", 0, 0, tiled=True)

    def block(step):
        return lax.dynamic_index_in_dim(total, (z // 4 + step) % 4, axis=0, keepdims=False)

    far = hop(block(2).astype(BF16), 0, -4)
    other = hop(block(1).astype(BF16), 1, 4)
    own = hop((block(0) + merger_bias).astype(BF16), 1, 0)
    near = (wide(block(3)) + wide(far)).astype(BF16)
    asked = hop(after(asked, near), -1, 0)
    near = hop(near, 1, -4)
    rows = (wide(own) + wide(other) + wide(near)).astype(BF16)
    rows, text, asked = lax.optimization_barrier((rows, text, asked))
    others = lax.ppermute(text, "core", [(0, 1), (1, 0)])
    return rows, text, others, asked


def soft(scores, live):
    scores = jnp.where(live, scores / math.sqrt(HD), MASKED)
    weights = jnp.exp(scores - jnp.max(scores, axis=-1, keepdims=True))
    return (weights / jnp.sum(weights, axis=-1, keepdims=True)).astype(BF16)


def project_kernel(
    length_ref, core_ref, counts_ref, starts_ref, mine_ref, others_ref, image_ref, bias_ref,
    cos_ref, sin_ref, asked_ref, weight_ref, cache_ref, fresh_ref,
):
    chunks, depth = 2 * mine_ref.shape[0], mine_ref.shape[2]
    rows = cache_ref.shape[0]
    images = image_ref.shape[0]
    widened = wide(image_ref[...])
    scaling = lax.rsqrt(jnp.sum(widened * widened, axis=1, keepdims=True) / D + EPSILON)
    position = lax.broadcasted_iota(jnp.int32, (rows, images), 0)
    source = lax.broadcasted_iota(jnp.int32, (rows, images), 1)
    picks = jnp.zeros((rows, images), F32)
    earlier = jnp.int32(0)
    for k in range(4):
        start, count = starts_ref[k], counts_ref[k]
        inside = (position >= start) & (position < start + count)
        chosen = inside & (source == position - start + earlier)
        picks = picks + jnp.where(chosen, 1.0, 0.0)
        earlier = earlier + count
    covered = jnp.sum(picks, axis=1, keepdims=True) > 0.5
    picks = picks.astype(BF16)
    core = core_ref[0]
    sides = ((mine_ref, core), (others_ref, 1 - core))
    squares = jnp.zeros((rows, 1), F32)
    for ref, side in sides:
        for row in range(chunks // 2):
            part = wide(ref[row, :rows, :])
            squares = squares + jnp.sum(part * part, axis=1, keepdims=True)
    text_scaling = lax.rsqrt(squares / D + EPSILON)
    text_total = jnp.zeros((rows, cache_ref.shape[1]), F32)
    image_total = jnp.zeros((images, cache_ref.shape[1]), F32)
    for row in range(chunks // 2):
        for ref, side in sides:
            chunk = 2 * row + side
            for first in range(0, depth, 256):
                part = slice(first, first + 256)
                columns = pl.ds(pl.multiple_of(chunk * depth + first, 256), 256)
                gain = wide(ref[row, rows:, part])[:1]
                weight = weight_ref[columns, :]
                normed = wide(ref[row, :rows, part]) * text_scaling * gain
                text_total = text_total + jnp.dot(
                    normed.astype(BF16), weight, preferred_element_type=F32
                )
                normed = wide(image_ref[:, columns]) * scaling * gain
                image_total = image_total + jnp.dot(
                    normed.astype(BF16), weight, preferred_element_type=F32
                )
    high = image_total.astype(BF16)
    rest = image_total - wide(high)
    middle = rest.astype(BF16)
    low = (rest - wide(middle)).astype(BF16)
    picked = jnp.dot(picks, high, preferred_element_type=F32)
    picked = picked + jnp.dot(picks, middle, preferred_element_type=F32)
    picked = picked + jnp.dot(picks, low, preferred_element_type=F32)
    projected = jnp.where(covered, picked, text_total) + bias_ref[...]
    keys = projected[:, :HD]
    turned = pltpu.roll(keys, HD // 2, axis=1)
    keys = (keys * cos_ref[...] + turned * sin_ref[...]).astype(BF16)
    values = projected[:, HD:].astype(BF16)
    cache_ref[:, :HD] = keys
    cache_ref[:, HD:] = values
    scores = lax.dot_general(
        asked_ref[...], keys, (((1,), (1,)), ((), ())), preferred_element_type=F32
    )
    live = lax.broadcasted_iota(jnp.int32, scores.shape, 1) < length_ref[0]
    mixed = jnp.dot(soft(scores, live), values, preferred_element_type=F32)
    fresh_ref[...] = mixed.astype(BF16)


def project(counts, starts, mine, others, images, weight, bias, asked, length):
    positions = mine.shape[1] - 16
    half = HD // 2
    frequency = THETA ** (-jnp.arange(half, dtype=F32) * 2.0 / HD)
    angles = jnp.arange(positions, dtype=F32)[:, None] * frequency[None, :]
    cosine, sine = jnp.cos(angles), jnp.sin(angles)
    cosine = jnp.concatenate([cosine, cosine], axis=1)
    sine = jnp.concatenate([-sine, sine], axis=1)
    columns = weight.shape[1]
    return pl.pallas_call(
        project_kernel,
        out_shape=(
            jax.ShapeDtypeStruct((positions, columns), BF16),
            jax.ShapeDtypeStruct(asked.shape, BF16),
        ),
        in_specs=[whole(pltpu.SMEM)] * 4 + [whole()] * 8,
        out_specs=(whole(), whole()),
        cost_estimate=SMALL,
        compiler_params=pltpu.CompilerParams(vmem_limit_bytes=VMEM_BYTES),
        name="project",
    )(
        length, lax.axis_index("core")[None], counts, starts, mine, others, images,
        bias[None, :], cosine, sine, asked, weight,
    )


def resident_kernel(tables_ref, lengths_ref, asked_ref, pages_ref, out_ref, scores_ref, mixed_ref):
    requests, pages = tables_ref.shape
    span = scores_ref.shape[1]
    positions = lax.broadcasted_iota(jnp.int32, (8, span), 1)

    def side(request, first):
        return jnp.concatenate(
            [
                pages_ref[tables_ref[request, k], :, first : first + HD]
                for k in range(pages)
            ],
            axis=0,
        )

    scores_ref[requests * 8 :, :] = jnp.zeros((8, span), F32)
    mixed_ref[requests * 8 :, :] = jnp.zeros((8, HD), F32)
    for request in range(requests):
        rows = pl.ds(request * 8, 8)
        scores = lax.dot_general(
            asked_ref[rows, :].astype(BF16),
            side(request, 0),
            (((1,), (1,)), ((), ())),
            preferred_element_type=F32,
        )
        scores_ref[rows, :] = jnp.where(
            positions < lengths_ref[request], scores / math.sqrt(HD), MASKED
        )
    scores = scores_ref[...]
    weights = jnp.exp(scores - jnp.max(scores, axis=-1, keepdims=True))
    scores_ref[...] = weights / jnp.sum(weights, axis=-1, keepdims=True)
    for request in range(requests):
        rows = pl.ds(request * 8, 8)
        mixed_ref[rows, :] = jnp.dot(
            scores_ref[rows, :].astype(BF16), side(request, HD), preferred_element_type=F32
        )
    out_ref[...] = mixed_ref[...].astype(BF16)


def attend_resident(queries, cache_pages, page_tables, context_lengths):
    heads = queries.size // HD
    span = page_tables.shape[1] * cache_pages.shape[1]
    out = pl.pallas_call(
        resident_kernel,
        out_shape=jax.ShapeDtypeStruct((heads, HD), BF16),
        in_specs=[whole(pltpu.SMEM), whole(pltpu.SMEM), whole(), whole()],
        out_specs=whole(),
        scratch_shapes=[pltpu.VMEM((heads, span), F32), pltpu.VMEM((heads, HD), F32)],
        cost_estimate=SMALL,
        compiler_params=pltpu.CompilerParams(vmem_limit_bytes=VMEM_BYTES),
        name="resident",
    )(page_tables, context_lengths, wide(queries).reshape(heads, HD), cache_pages)
    return out


def per_device(
    merged_hidden,
    merger_weight,
    merger_bias,
    text_embed,
    image_tokens,
    image_offsets,
    prefill_gain,
    kv_weight,
    kv_bias,
    prompt_lengths,
    queries,
    cache_pages,
    page_tables,
    context_lengths,
):
    weight = lax.all_gather(kv_weight, "seq", axis=0, tiled=True)
    *shares, text = merger_shares(merged_hidden, merger_weight, text_embed, prefill_gain)
    resident = queries.shape[0] - 1
    asked = queries[resident:].reshape(-1, HD)
    image_rows, text, others, asked = summed_images(shares, merger_bias, text, asked)
    image_all = lax.all_gather(image_rows, TP, axis=1, tiled=True)
    resident_out = attend_resident(queries, cache_pages, page_tables, context_lengths)
    place = lax.axis_index("section") * lax.axis_size("seq") + lax.axis_index("seq")
    length = lax.dynamic_slice_in_dim(prompt_lengths, place, 1, 0)
    prompt_cache, fresh = project(
        image_tokens[0], image_offsets[0], text, others, image_all, weight, kv_bias, asked, length
    )
    fresh_out = hop(fresh, 1, 0).reshape(1, -1)
    last = jnp.arange(resident + 1, dtype=jnp.int32)[:, None] == resident
    decode_out = jnp.where(last, fresh_out, resident_out.reshape(queries.shape))
    return (prompt_cache, decode_out)


def solution(mesh):
    sections, owners, columns = mesh.devices.shape
    devices = mesh.devices.reshape(sections, owners, columns // 2, 2)
    mesh = jax.sharding.Mesh(devices, ("section", "seq") + TP)
    return jax.shard_map(
        per_device,
        mesh=mesh,
        in_specs=(
            P("section", "seq"),
            P("seq", TP),
            P(TP),
            P(("section", "seq"), TP),
            P(("section", "seq"), None),
            P(("section", "seq"), None),
            P(TP),
            P("seq", TP),
            P(TP),
            P(),
            P(("section", "seq"), TP),
            P(("section", "seq"), None, TP),
            P(("section", "seq"), None),
            P(("section", "seq")),
        ),
        out_specs=(P(("section", "seq"), TP), P(("section", "seq"), TP)),
        check_vma=False,
    )
```
